32 devices in a mesh: dom: 16 (over z, y, x), depth: 2 (over core).
Axes of the slice: x: 2, y: 2, z: 4, core: 2. Of those that a mesh axis runs over, the one named last changes fastest.
Arguments:
- ancestors: int32 [16], P('dom'), may hold values from 0 to 15, as said below
- ensemble: float32 [16, 4, 12, 16, 128], P('dom', None, 'depth'), may hold values from -4 to 4
- diffusivity: float32 [12, 16, 128], P('depth'), may hold values from 0.02 to 0.1
- melting_speed: float32 [12, 16, 128], P('depth'), may hold values from 0.05 to 0.3
- permeability: float32 [12, 16, 128], P('depth'), may hold values from 0.5 to 2
Outputs:
- forecast_ensemble: float32 [16, 4, 12, 16, 128], P('dom', None, 'depth')
The draws below stay inside these ranges and needn't reach their ends.
Inputs may be any that keep to these rules, and one draw needn't show every extreme that they name: `ancestors`: each entry names a particle; slots 0 and 2 descend from particle 1, slot 1 from particle 0, slot 3 from particle 16 - 1.
All inputs are finite; a program needn't handle non-finite values.
Results may differ from the reference program's by a relative error of at most 0.00002.
Values sent between devices are 32-bit elements; how exact they have to be, the bound alone decides.
No kernel may reach another device: no remote copies, remote signals or barrier semaphores. Data moves between devices by JAX's collectives and lax.ppermute only.
A program may use at most 64 MiB of HBM per device.

```python
import math
import jax
import jax.numpy as jnp
from jax import lax

FIELDS = 4
NX = 16
NY = 128
STEPS = 4
PARTICLES = 16
NZ = 12


def draw_ancestors(key, part):
    key_perm = jax.random.fold_in(key, 11)
    key_first = jax.random.fold_in(key, 12)
    key_second = jax.random.fold_in(key, 13)
    order = jax.random.permutation(key_perm, PARTICLES).astype(jnp.int32)
    first = jax.random.randint(key_first, (PARTICLES,), 0, PARTICLES, dtype=jnp.int32)
    second = jax.random.randint(key_second, (PARTICLES,), 0, PARTICLES, dtype=jnp.int32)
    picked = order[jnp.minimum(first, second)]
    picked = picked.at[0].set(1)
    picked = picked.at[1].set(0)
    picked = picked.at[2].set(1)
    picked = picked.at[3].set(PARTICLES - 1)
    return picked.astype(jnp.int32)


def block_scale(key, shape, shards, smallest, high):
    gain = 1.0
    for axis_at, blocks in shards:
        steps = jax.random.uniform(jax.random.fold_in(jax.random.fold_in(key, 6), axis_at), (blocks,), jnp.float32, smallest / len(shards), high / len(shards))
        gain = gain * jnp.repeat(jnp.exp(steps), shape[axis_at] // blocks).reshape((-1,) + (1,) * (len(shape) - 1 - axis_at))
    return gain


def normal_values(rng, shape, deviation, limit, cuts=(), kind=jnp.bfloat16):
    entries = jax.random.normal(rng, shape, jnp.float32) * deviation
    if len(cuts) > 0:
        entries = block_scale(rng, shape, cuts, -0.22, 0.18) * entries
    return jnp.clip(entries, min=-limit, max=limit).astype(kind)


def setup_inputs(seed: int = 0) -> dict:
    splits = jax.random.split(jax.random.key(seed), 6)
    ancestors = draw_ancestors(jax.random.fold_in(splits[5], 71), 0)
    ensemble = normal_values(splits[1], (PARTICLES, FIELDS, NZ, NX, NY), 1.0, 4.0, ((0, 16), (2, 2)), jnp.float32)
    diffusivity = jnp.clip(jnp.exp(math.log(0.1) - 1.609438 * jax.random.uniform(splits[2], (NZ, NX, NY), jnp.float32) ** block_scale(splits[2], (NZ, NX, NY), ((0, 2),), -0.2, 0.2)), 0.02, 0.1)
    melting_speed = jnp.clip(jnp.exp(math.log(0.3) - 1.7917595 * jax.random.uniform(splits[3], (NZ, NX, NY), jnp.float32) ** block_scale(splits[3], (NZ, NX, NY), ((0, 2),), -0.2, 0.2)), 0.05, 0.3)
    permeability = jnp.clip(jnp.exp(math.log(2.0) - 1.3862944 * jax.random.uniform(splits[4], (NZ, NX, NY), jnp.float32) ** block_scale(splits[4], (NZ, NX, NY), ((0, 2),), -0.2, 0.2)), 0.5, 2.0)
    return dict(ancestors=ancestors, ensemble=ensemble, diffusivity=diffusivity, melting_speed=melting_speed, permeability=permeability)


advect_coef = 0.1


def advance(padded, diffuse, reacts, permeab):
    center = padded[:, :, 1:-1]
    upper_cells = padded[:, :, :-2]
    lower_cells = padded[:, :, 2:]
    flat_pad = jnp.pad(center, ((0, 0), (0, 0), (0, 0), (1, 1), (1, 1)))
    laplacian_operator = upper_cells + lower_cells + flat_pad[:, :, :, 2:, 1:-1] + flat_pad[:, :, :, :-2, 1:-1]
    laplacian_operator = laplacian_operator + flat_pad[:, :, :, 1:-1, 2:] + flat_pad[:, :, :, 1:-1, :-2] - 6.0 * center
    velocity = center[:, 1]
    transport_update = advect_coef * jnp.maximum(velocity, 0.0)[:, None] * (center - upper_cells)
    transport_update = transport_update + advect_coef * jnp.minimum(velocity, 0.0)[:, None] * (lower_cells - center)
    fraction = center[:, 0]
    enthalpy = center[:, 2]
    composition = center[:, 3]
    melting = reacts * (enthalpy - 0.5 * composition)
    new_fraction = fraction - transport_update[:, 0] + melting
    new_velocity = velocity + 0.2 * (permeab * jnp.tanh(fraction) - velocity) + 0.1 * laplacian_operator[:, 1]
    new_enthalpy = enthalpy - transport_update[:, 2] + diffuse * laplacian_operator[:, 2] - 0.5 * melting
    new_composition = composition - transport_update[:, 3] + diffuse * laplacian_operator[:, 3]
    return jnp.stack([new_fraction, new_velocity, new_enthalpy, new_composition], axis=1)


def reference(ancestors, ensemble, diffusivity, melting_speed, permeability):
    present_members = jnp.take(ensemble, ancestors.astype(jnp.int32), axis=0)

    def one_step(step_index, field_stack):
        padded = jnp.pad(field_stack, ((0, 0), (0, 0), (1, 1), (0, 0), (0, 0)))
        return advance(padded, diffusivity, melting_speed, permeability)

    return lax.fori_loop(0, STEPS, one_step, present_members)
```

```python
import functools

import jax
import jax.numpy as jnp
from jax import lax
from jax.experimental import pallas as pl
from jax.experimental.pallas import tpu as pltpu
from jax.sharding import PartitionSpec as P

STEPS = 4
ADVECT = 0.1
SMEM = pl.BlockSpec(memory_space=pltpu.SMEM)
VMEM = pl.BlockSpec(memory_space=pltpu.VMEM)


def neighbours(q):
    rows = lax.broadcasted_iota(jnp.int32, q.shape, 0)
    columns = lax.broadcasted_iota(jnp.int32, q.shape, 1)
    high_row, high_column = q.shape[0] - 1, q.shape[1] - 1
    total = jnp.where(rows == 0, 0.0, pltpu.roll(q, 1, 0))
    total = total + jnp.where(rows == high_row, 0.0, pltpu.roll(q, high_row, 0))
    total = total + jnp.where(columns == 0, 0.0, pltpu.roll(q, 1, 1))
    return total + jnp.where(columns == high_column, 0.0, pltpu.roll(q, high_column, 1))


def layer_step(state, layer, diffuse, reacts, permeab):
    m, v, h, c = (state[q, layer] for q in range(4))
    m_up, v_up, h_up, c_up = (state[q, layer - 1] for q in range(4))
    m_low, v_low, h_low, c_low = (state[q, layer + 1] for q in range(4))
    down = ADVECT * jnp.maximum(v, 0.0)
    up = ADVECT * jnp.minimum(v, 0.0)

    def transport(q, upper, lower):
        return down * (q - upper) + up * (lower - q)

    def laplace(q, upper, lower):
        return upper + lower + neighbours(q) - 6.0 * q

    melting = reacts * (h - 0.5 * c)
    return (
        m - transport(m, m_up, m_low) + melting,
        v + 0.2 * (permeab * jnp.tanh(m) - v) + 0.1 * laplace(v, v_up, v_low),
        h - transport(h, h_up, h_low) + diffuse * laplace(h, h_up, h_low) - 0.5 * melting,
        c - transport(c, c_up, c_low) + diffuse * laplace(c, c_up, c_low),
    )


def forecast_kernel(
    cells, pair, place_ref, own, low, high, own_d, low_d, high_d, own_r, low_r, high_r, own_p, low_p, high_p,
    a_ref, b_ref, even, odd, coefs,
):
    place = place_ref[0]
    window = cells + (STEPS if pair else 2 * STEPS)
    zero = jnp.zeros(even.shape[2:], jnp.float32)
    for q in range(4):
        for buffer in (even, odd):
            buffer[q, 0] = zero
            buffer[q, window + 1] = zero

    def fill(at, start, source, first):
        for i in range(first[1]):
            for q in range(4):
                even[q, at + i] = source[0][0, q, start + i]
            for q in range(3):
                coefs[q, at + i] = source[1 + q][start + i]

    mine, lows, highs = (own, own_d, own_r, own_p), (low, low_d, low_r, low_p), (high, high_d, high_r, high_p)
    if pair:
        first = place == 0
        fill(jnp.where(first, 1, 1 + STEPS), 0, mine, (0, cells))
        fill(jnp.where(first, 1 + cells, 1), jnp.where(first, 0, cells - STEPS), lows, (0, STEPS))
    else:
        fill(1, cells - STEPS, lows, (0, STEPS))
        fill(1 + STEPS, 0, mine, (0, cells))
        fill(1 + STEPS + cells, 0, highs, (0, STEPS))
        inside_first = jnp.where(place == 0, 1 + STEPS, 0)
        inside_last = jnp.where(place == 2, STEPS + cells, window + 1)

    buffers = (even, odd)
    for step in range(STEPS):
        now, later = buffers[step % 2], buffers[1 - step % 2]
        left = STEPS - 1 - step
        if pair:
            start, count = jnp.where(first, 1, 2 + step), cells + left
        else:
            start, count = 2 + step, cells + 2 * left
        for i in range(count):
            layer = start + i
            values = layer_step(now, layer, coefs[0, layer], coefs[1, layer], coefs[2, layer])
            if step == STEPS - 1:
                a_ref[0, i], a_ref[1, i], b_ref[0, i], b_ref[1, i] = values
            else:
                for q in range(4):
                    value = values[q]
                    if not pair:
                        value = jnp.where((layer >= inside_first) & (layer <= inside_last), value, 0.0)
                    later[q, layer] = value


def forecast(ensemble, diffusivity, melting_speed, permeability):
    count = lax.axis_size("depth")
    arrays = (ensemble, diffusivity, melting_speed, permeability)
    pair = count == 2
    at = lax.axis_index("depth")
    if pair:
        swapped = [lax.ppermute(x, "depth", [(0, 1), (1, 0)]) for x in arrays]
        lows, highs, place = swapped, swapped, at
    else:
        up = [(i, i + 1) for i in range(count - 1)]
        lows = [lax.ppermute(x, "depth", up) for x in arrays]
        highs = [lax.ppermute(x, "depth", [(j, i) for i, j in up]) for x in arrays]
        place = jnp.where(at == 0, 0, jnp.where(at == count - 1, 2, 1))
    cells, rows, columns = diffusivity.shape
    window = cells + (STEPS if pair else 2 * STEPS)
    half = jax.ShapeDtypeStruct((2, cells, rows, columns), jnp.float32)
    operands = [x for group in zip(arrays, lows, highs) for x in group]
    return pl.pallas_call(
        functools.partial(forecast_kernel, cells, pair),
        out_shape=(half, half),
        in_specs=[SMEM] + [VMEM] * len(operands),
        out_specs=(VMEM, VMEM),
        scratch_shapes=[
            pltpu.VMEM((4, window + 2, rows, columns), jnp.float32),
            pltpu.VMEM((4, window + 2, rows, columns), jnp.float32),
            pltpu.VMEM((3, window + 2, rows, columns), jnp.float32),
        ],
        compiler_params=pltpu.CompilerParams(vmem_limit_bytes=16 * 1024 * 1024),
        name="forecast",
    )(place.reshape(1).astype(jnp.int32), *operands)


def choose_kernel(count, outputs, wanted, *refs):
    candidates, results = refs[:count], refs[count:]
    for j in range(outputs):
        for k in range(count):

            @pl.when(wanted[j] == k)
            def _(j=j, k=k):
                results[j][...] = candidates[k][...]


def choose(candidates, wanted, name):
    outputs = wanted.shape[0]
    one = jax.ShapeDtypeStruct(candidates[0].shape, jnp.float32)
    return pl.pallas_call(
        functools.partial(choose_kernel, len(candidates), outputs),
        out_shape=[one] * outputs,
        in_specs=[SMEM] + [VMEM] * len(candidates),
        out_specs=[VMEM] * outputs,
        compiler_params=pltpu.CompilerParams(vmem_limit_bytes=16 * 1024 * 1024),
        name=name,
    )(wanted, *candidates)


def finish_kernel(count, wanted, *refs):
    a_parts, b_parts, out = refs[:count], refs[count : -1], refs[-1]
    for k in range(count):

        @pl.when(wanted[0] == k)
        def _(k=k):
            out[0, 0:2] = a_parts[k][...]

    for k in range(len(b_parts)):

        @pl.when(wanted[1] == k)
        def _(k=k):
            out[0, 2:4] = b_parts[k][...]


def swap(x, distance):
    return lax.ppermute(x, "dom", [(i, i ^ distance) for i in range(lax.axis_size("dom"))])


def resample(ancestors, a, b):
    count = lax.axis_size("dom")
    me = lax.axis_index("dom")
    bits = count.bit_length() - 1
    inner = 1 << (bits // 2)
    outer = count // inner
    near, far = range(1, inner), range(1, outer)
    mine = ancestors.reshape(1)
    far_ancestors = [mine] + [swap(mine, j * inner) for j in far]
    near_ancestors = [mine] + [swap(mine, k) for k in near]
    b_got = [b] + [swap(b, j * inner) for j in far]
    a_got = [a] + [swap(a, k) for k in near]
    a_wanted = (jnp.concatenate(far_ancestors) ^ me) & (inner - 1)
    a_sent = choose(a_got, a_wanted, "choose_place")
    a_final = [a_sent[0]] + [swap(a_sent[j], j * inner) for j in far]
    b_wanted = (jnp.concatenate(near_ancestors) ^ me) // inner
    b_sent = choose(b_got, b_wanted, "choose_column")
    b_final = [b_sent[0]] + [swap(b_sent[k], k) for k in near]
    last = jnp.concatenate([(mine ^ me) // inner, (mine ^ me) & (inner - 1)])
    return pl.pallas_call(
        functools.partial(finish_kernel, outer),
        out_shape=jax.ShapeDtypeStruct((1, 4) + a.shape[1:], jnp.float32),
        in_specs=[SMEM] + [VMEM] * (outer + inner),
        out_specs=VMEM,
        compiler_params=pltpu.CompilerParams(vmem_limit_bytes=16 * 1024 * 1024),
        name="finish",
    )(last, *a_final, *b_final)


def local(ancestors, ensemble, diffusivity, melting_speed, permeability):
    a, b = forecast(ensemble, diffusivity, melting_speed, permeability)
    return resample(ancestors, a, b)


def solution(mesh):
    return jax.shard_map(
        local,
        mesh=mesh,
        in_specs=(
            P("dom"),
            P("dom", None, "depth", None, None),
            P("depth", None, None),
            P("depth", None, None),
            P("depth", None, None),
        ),
        out_specs=P("dom", None, "depth", None, None),
        check_vma=False,
    )
```

```python
import functools

import jax
import jax.numpy as jnp
from jax import lax
from jax.experimental import pallas as pl
from jax.experimental.pallas import tpu as pltpu
from jax.sharding import PartitionSpec as P

STEPS = 4
ORDER = (1, 2, 3), (1, 2, 3)
ADVECT = 0.1
SMEM = pl.BlockSpec(memory_space=pltpu.SMEM)
VMEM = pl.BlockSpec(memory_space=pltpu.VMEM)
LIMIT = pltpu.CompilerParams(vmem_limit_bytes=32 * 1024 * 1024)


def neighbours(q):
    rows = lax.broadcasted_iota(jnp.int32, q.shape, 0)
    columns = lax.broadcasted_iota(jnp.int32, q.shape, 1)
    high_row, high_column = q.shape[0] - 1, q.shape[1] - 1
    total = jnp.where(rows == 0, 0.0, pltpu.roll(q, 1, 0))
    total = total + jnp.where(rows == high_row, 0.0, pltpu.roll(q, high_row, 0))
    total = total + jnp.where(columns == 0, 0.0, pltpu.roll(q, 1, 1))
    return total + jnp.where(columns == high_column, 0.0, pltpu.roll(q, high_column, 1))


def layer_step(state, layer, diffuse, reacts, permeab):
    m, v, h, c = (state[q, layer] for q in range(4))
    m_up, v_up, h_up, c_up = (state[q, layer - 1] for q in range(4))
    m_low, v_low, h_low, c_low = (state[q, layer + 1] for q in range(4))
    down = ADVECT * jnp.maximum(v, 0.0)
    up = ADVECT * jnp.minimum(v, 0.0)

    def transport(q, upper, lower):
        return down * (q - upper) + up * (lower - q)

    def laplace(q, upper, lower):
        return upper + lower + neighbours(q) - 6.0 * q

    melting = reacts * (h - 0.5 * c)
    return (
        m - transport(m, m_up, m_low) + melting,
        v + 0.2 * (permeab * jnp.tanh(m) - v) + 0.1 * laplace(v, v_up, v_low),
        h - transport(h, h_up, h_low) + diffuse * laplace(h, h_up, h_low) - 0.5 * melting,
        c - transport(c, c_up, c_low) + diffuse * laplace(c, c_up, c_low),
    )


def forecast_kernel(cells, pair, count, *refs):
    own, own_coefs, low, high = refs[0], refs[1:4], refs[4], refs[5]
    out, even, odd, coefs = refs[6:]
    at = lax.axis_index("depth")
    window = cells + (STEPS if pair else 2 * STEPS)
    zero = jnp.zeros(even.shape[2:], jnp.float32)
    for q in range(4):
        for buffer in (even, odd):
            buffer[q, 0] = zero
            buffer[q, window + 1] = zero

    def fill(to, layers, state):
        for i in range(layers):
            for q in range(7):
                (even if q < 4 else coefs)[q % 4, to + i] = state(q, i)

    def mine(q, i):
        return own[0, q, i] if q < 4 else own_coefs[q - 4][i]

    if pair:
        first = at == 0
        fill(jnp.where(first, 1, 1 + STEPS), cells, mine)
        fill(jnp.where(first, 1 + cells, 1), STEPS, lambda q, i: low[q, i])
    else:
        fill(1, STEPS, lambda q, i: low[q, i])
        fill(1 + STEPS, cells, mine)
        fill(1 + STEPS + cells, STEPS, lambda q, i: high[q, i])
        inside_first = jnp.where(at == 0, 1 + STEPS, 0)
        inside_last = jnp.where(at == count - 1, STEPS + cells, window + 1)

    buffers = (even, odd)
    for step in range(STEPS):
        now, later = buffers[step % 2], buffers[1 - step % 2]
        left = STEPS - 1 - step
        if pair:
            start, layers = jnp.where(first, 1, 2 + step), cells + left
        else:
            start, layers = 2 + step, cells + 2 * left
        for i in range(layers):
            layer = start + i
            values = layer_step(now, layer, coefs[0, layer], coefs[1, layer], coefs[2, layer])
            for q in range(4):
                value = values[q]
                if step == STEPS - 1:
                    out[0, q, i] = value
                    continue
                if not pair:
                    value = jnp.where((layer >= inside_first) & (layer <= inside_last), value, 0.0)
                later[q, layer] = value


def other_side(x, towards):
    count = lax.axis_size("depth")
    if count == 2:
        return lax.ppermute(x, "depth", [(0, 1), (1, 0)])
    return lax.ppermute(x, "depth", [(i, i + towards) for i in range(count) if 0 <= i + towards < count])


def forecast(state, edges, coefs):
    count = lax.axis_size("depth")
    pair = count == 2
    _, _, cells, rows, columns = state.shape
    window = cells + (STEPS if pair else 2 * STEPS)
    if pair:
        low = high = other_side(edges[0], 1)
    else:
        low, high = other_side(edges[1], 1), other_side(edges[0], -1)
    return pl.pallas_call(
        functools.partial(forecast_kernel, cells, pair, count),
        out_shape=jax.ShapeDtypeStruct(state.shape, jnp.float32),
        in_specs=[VMEM] * 6,
        out_specs=VMEM,
        scratch_shapes=[
            pltpu.VMEM((4, window + 2, rows, columns), jnp.float32),
            pltpu.VMEM((4, window + 2, rows, columns), jnp.float32),
            pltpu.VMEM((3, window + 2, rows, columns), jnp.float32),
        ],
        compiler_params=LIMIT,
        name="forecast",
    )(state, *coefs, low, high)


def first_wishes_kernel(mine, other, out):
    rows = lax.broadcasted_iota(jnp.int32, out.shape, 0)
    pair = [jnp.broadcast_to(x[...].reshape(1, 1), out.shape) for x in (mine, other)]
    out[...] = jnp.where(rows == 0, pair[0], pair[1])


def join_wishes_kernel(known, mine, other, out):
    rows = lax.broadcasted_iota(jnp.int32, out.shape, 0)
    out[...] = jnp.where(rows < known, mine[...], pltpu.roll(other[...], known, 0))


def hop(wish, sides, phase):
    offset = wish ^ lax.axis_index("dom")
    inner = offset & (sides - 1)
    outer = lax.shift_right_logical(offset, sides.bit_length() - 1)
    return jnp.where(lax.axis_index("depth") % 2 == phase, inner, outer)


def tiles(shape):
    return [(0, q, i, slice(r, r + 8)) for q in range(shape[1]) for i in range(shape[2]) for r in range(0, shape[3], 8)]


def pick(values, masks):
    value = values[0]
    for mask, other in zip(masks, values[1:]):
        value = jnp.where(mask, other, value)
    return value


def masks_of(wish, sides, phase):
    wanted = jnp.broadcast_to(hop(wish, sides, phase), (8, wish.shape[-1]))
    return [wanted == k for k in range(1, sides)]


def near_kernel(sides, wishes, state, out):
    out[...] = hop(wishes[...], sides, 0)


def choose_kernel(sides, *refs):
    candidates, near, far, results = refs[:sides], refs[sides], refs[sides + 1], refs[sides + 2 :]
    half = sides // 2
    wanted = near[...], hop(far[...], sides, 0)
    masks = [
        [jnp.broadcast_to(wanted[j // half][j % half : j % half + 1], near.shape) == k for k in range(1, sides)]
        for j in range(sides)
    ]
    for at in tiles(candidates[0].shape):
        values = [candidate[at] for candidate in candidates]
        for j in range(sides):
            results[j][at] = pick(values, masks[j])


def settle_kernel(sides, pair, *refs):
    candidates, wishes, coefs = refs[:sides], refs[sides], refs[sides + 1 : sides + 4]
    result, edges = refs[sides + 4], refs[sides + 5 :]
    masks = masks_of(wishes[0:1], sides, 1)
    for at in tiles(result.shape):
        result[at] = pick([candidate[at] for candidate in candidates], masks)
    cells = result.shape[2]
    starts = [jnp.where(lax.axis_index("depth") == 0, cells - STEPS, 0)] if pair else [0, cells - STEPS]
    for start, edge in zip(starts, edges):
        for q in range(4):
            edge[q] = result[0, q, pl.ds(start, STEPS)]
        for q in range(3):
            edge[4 + q] = coefs[q][pl.ds(start, STEPS)]


def swap(x, distance, phase):
    count, depth = lax.axis_size("dom"), lax.axis_size("depth")
    sides = 1 << (count.bit_length() // 2)
    pairs = []
    for i in range(count):
        for d in range(depth):
            pairs.append((i * depth + d, (i ^ (distance if d % 2 == phase else distance * sides)) * depth + d))
    return lax.ppermute(x, ("dom", "depth"), pairs)


def local(ancestors, ensemble, diffusivity, melting_speed, permeability):
    count, depth = lax.axis_size("dom"), lax.axis_size("depth")
    sides = 1 << (count.bit_length() // 2)
    assert sides * sides == count
    far = range(1, sides)
    like = jax.ShapeDtypeStruct(ensemble.shape, jnp.float32)
    other = swap(ancestors, 1, 1)
    first, second = ORDER if sides == 4 else (far, far)
    got = {k: swap(ensemble, k, 0) for k in first}
    coefs = (diffusivity, melting_speed, permeability)
    wishes = pl.pallas_call(
        first_wishes_kernel,
        out_shape=jax.ShapeDtypeStruct((8, ensemble.shape[-1]), jnp.int32),
        in_specs=[VMEM] * 2,
        out_specs=VMEM,
        compiler_params=LIMIT,
        name="first_wishes",
    )(ancestors, other)
    known = 2
    while 2 * known < sides:
        wishes = pl.pallas_call(
            functools.partial(join_wishes_kernel, known),
            out_shape=jax.ShapeDtypeStruct(wishes.shape, jnp.int32),
            in_specs=[VMEM] * 2,
            out_specs=VMEM,
            compiler_params=LIMIT,
            name="join_wishes",
        )(wishes, swap(wishes, known, 1))
        known *= 2
    far_wishes = swap(wishes, known, 1)
    near = pl.pallas_call(
        functools.partial(near_kernel, sides),
        out_shape=jax.ShapeDtypeStruct(wishes.shape, jnp.int32),
        in_specs=[VMEM] * 2,
        out_specs=VMEM,
        compiler_params=LIMIT,
        name="near",
    )(wishes, ensemble)
    sent = pl.pallas_call(
        functools.partial(choose_kernel, sides),
        out_shape=[like] * sides,
        in_specs=[VMEM] * (sides + 2),
        out_specs=[VMEM] * sides,
        compiler_params=LIMIT,
        name="choose",
    )(ensemble, *(got[k] for k in far), near, far_wishes)
    final = {k: swap(sent[k], k, 1) for k in second}
    edge = jax.ShapeDtypeStruct((7, STEPS) + ensemble.shape[3:], jnp.float32)
    edges = [edge] if depth == 2 else [edge, edge]
    state, *edges = pl.pallas_call(
        functools.partial(settle_kernel, sides, depth == 2),
        out_shape=[like] + edges,
        in_specs=[VMEM] * (sides + 4),
        out_specs=[VMEM] * (1 + len(edges)),
        compiler_params=LIMIT,
        name="settle",
    )(sent[0], *(final[k] for k in far), wishes, *coefs)
    return forecast(state, edges, coefs)


def solution(mesh):
    return jax.shard_map(
        local,
        mesh=mesh,
        in_specs=(
            P("dom"),
            P("dom", None, "depth", None, None),
            P("depth", None, None),
            P("depth", None, None),
            P("depth", None, None),
        ),
        out_specs=P("dom", None, "depth", None, None),
        check_vma=False,
    )
```

```python
import functools
import itertools
import operator

import jax
import jax.numpy as jnp
from jax import lax
from jax.experimental import pallas as pl
from jax.experimental.pallas import tpu as pltpu
from jax.sharding import PartitionSpec as P

STEPS = 4
ADVECT = 0.1
SMEM = pl.BlockSpec(memory_space=pltpu.SMEM)
VMEM = pl.BlockSpec(memory_space=pltpu.VMEM)
FIRST_HOP = pl.CostEstimate(flops=10**10, bytes_accessed=8 * 10**6, transcendentals=0)
LIMIT = pltpu.CompilerParams(vmem_limit_bytes=32 * 1024 * 1024)


def neighbours(q):
    rows = lax.broadcasted_iota(jnp.int32, q.shape, 0)
    columns = lax.broadcasted_iota(jnp.int32, q.shape, 1)
    high_row, high_column = q.shape[0] - 1, q.shape[1] - 1
    total = jnp.where(rows == 0, 0.0, pltpu.roll(q, 1, 0))
    total = total + jnp.where(rows == high_row, 0.0, pltpu.roll(q, high_row, 0))
    total = total + jnp.where(columns == 0, 0.0, pltpu.roll(q, 1, 1))
    return total + jnp.where(columns == high_column, 0.0, pltpu.roll(q, high_column, 1))


def layer_step(state, layer, diffuse, reacts, permeab):
    m, v, h, c = (state[q, layer] for q in range(4))
    m_up, v_up, h_up, c_up = (state[q, layer - 1] for q in range(4))
    m_low, v_low, h_low, c_low = (state[q, layer + 1] for q in range(4))
    down = ADVECT * jnp.maximum(v, 0.0)
    up = ADVECT * jnp.minimum(v, 0.0)

    def transport(q, upper, lower):
        return down * (q - upper) + up * (lower - q)

    def laplace(q, upper, lower):
        return upper + lower + neighbours(q) - 6.0 * q

    melting = reacts * (h - 0.5 * c)
    return (
        m - transport(m, m_up, m_low) + melting,
        v + 0.2 * (permeab * jnp.tanh(m) - v) + 0.1 * laplace(v, v_up, v_low),
        h - transport(h, h_up, h_low) + diffuse * laplace(h, h_up, h_low) - 0.5 * melting,
        c - transport(c, c_up, c_low) + diffuse * laplace(c, c_up, c_low),
    )


def forecast_kernel(cells, pair, count, *refs):
    own, own_coefs, low, high = refs[0], refs[1:4], refs[4], refs[5]
    out, even, odd, coefs = refs[6:]
    at = lax.axis_index("depth")
    window = cells + (STEPS if pair else 2 * STEPS)
    zero = jnp.zeros(even.shape[2:], jnp.float32)
    for q in range(4):
        for buffer in (even, odd):
            buffer[q, 0] = zero
            buffer[q, window + 1] = zero

    def fill(to, layers, state):
        for i in range(layers):
            for q in range(7):
                (even if q < 4 else coefs)[q % 4, to + i] = state(q, i)

    def mine(q, i):
        return own[0, q, i] if q < 4 else own_coefs[q - 4][i]

    if pair:
        first = at == 0
        fill(jnp.where(first, 1, 1 + STEPS), cells, mine)
        fill(jnp.where(first, 1 + cells, 1), STEPS, lambda q, i: low[q, i])
    else:
        fill(1, STEPS, lambda q, i: low[q, i])
        fill(1 + STEPS, cells, mine)
        fill(1 + STEPS + cells, STEPS, lambda q, i: high[q, i])
        inside_first = jnp.where(at == 0, 1 + STEPS, 0)
        inside_last = jnp.where(at == count - 1, STEPS + cells, window + 1)

    buffers = (even, odd)
    for step in range(STEPS):
        now, later = buffers[step % 2], buffers[1 - step % 2]
        left = STEPS - 1 - step
        if pair:
            start, layers = jnp.where(first, 1, 2 + step), cells + left
        else:
            start, layers = 2 + step, cells + 2 * left
        for i in range(layers):
            layer = start + i
            values = layer_step(now, layer, coefs[0, layer], coefs[1, layer], coefs[2, layer])
            for q in range(4):
                value = values[q]
                if step == STEPS - 1:
                    out[0, q, i] = value
                    continue
                if not pair:
                    value = jnp.where((layer >= inside_first) & (layer <= inside_last), value, 0.0)
                later[q, layer] = value


def other_side(x, towards):
    count = lax.axis_size("depth")
    if count == 2:
        return lax.ppermute(x, "depth", [(0, 1), (1, 0)])
    return lax.ppermute(x, "depth", [(i, i + towards) for i in range(count) if 0 <= i + towards < count])


def forecast(state, edges, coefs):
    count = lax.axis_size("depth")
    pair = count == 2
    _, _, cells, rows, columns = state.shape
    window = cells + (STEPS if pair else 2 * STEPS)
    if pair:
        low = high = other_side(edges[0], 1)
    else:
        low, high = other_side(edges[1], 1), other_side(edges[0], -1)
    return pl.pallas_call(
        functools.partial(forecast_kernel, cells, pair, count),
        out_shape=jax.ShapeDtypeStruct(state.shape, jnp.float32),
        in_specs=[VMEM] * 6,
        out_specs=VMEM,
        scratch_shapes=[
            pltpu.VMEM((4, window + 2, rows, columns), jnp.float32),
            pltpu.VMEM((4, window + 2, rows, columns), jnp.float32),
            pltpu.VMEM((3, window + 2, rows, columns), jnp.float32),
        ],
        compiler_params=LIMIT,
        name="forecast",
    )(state, *coefs, low, high)


def first_wishes_kernel(mine, out):
    out[...] = jnp.full(out.shape, mine[0], jnp.int32)


def ways_of(phase):
    half = (lax.axis_size("dom").bit_length() - 1) // 2
    low = [1 << bit for bit in range(half)]
    high = [step << half for step in low]
    even, odd = (low[::-1], list(itertools.accumulate(high, operator.or_))) if phase == 0 else (high[::-1], low)
    ways = []
    for basis in (even, odd):
        offsets = [0]
        for step in basis:
            offsets += [offset ^ step for offset in offsets]
        ways.append(offsets)
    return ways


def hop_masks(wish, phase):
    even, odd = ways_of(phase)
    first = lax.axis_index("depth") % 2 == 0
    covered = jnp.where(first, functools.reduce(operator.or_, even), functools.reduce(operator.or_, odd))
    offset = (wish ^ lax.axis_index("dom")) & covered
    return [offset == jnp.where(first, *pair) for pair in list(zip(even, odd))[1:]]


def tiles(shape):
    return [(0, q, i, slice(r, r + 8)) for q in range(shape[1]) for i in range(shape[2]) for r in range(0, shape[3], 8)]


def pick(values, masks):
    value = values[0]
    for mask, other in zip(masks, values[1:]):
        value = jnp.where(mask, other, value)
    return value


def choose_kernel(sides, *refs):
    candidates, rest = refs[:sides], refs[sides:]
    wishes, results = rest[: len(rest) // 2], rest[len(rest) // 2 :]
    masks = [hop_masks(wish[...], 0) for wish in wishes]
    for at in tiles(candidates[0].shape):
        values = [candidate[at] for candidate in candidates]
        for mask, result in zip(masks, results):
            result[at] = pick(values, mask)


def choose(candidates, wishes):
    sides, outputs = len(candidates), len(wishes)
    return pl.pallas_call(
        functools.partial(choose_kernel, sides),
        out_shape=[jax.ShapeDtypeStruct(candidates[0].shape, jnp.float32)] * outputs,
        in_specs=[VMEM] * (sides + outputs),
        out_specs=[VMEM] * outputs,
        compiler_params=LIMIT,
        name="choose",
    )(*candidates, *wishes)


def settle_kernel(sides, pair, *refs):
    candidates, wishes, coefs = refs[:sides], refs[sides], refs[sides + 1 : sides + 4]
    result, edges = refs[sides + 4], refs[sides + 5 :]
    masks = hop_masks(wishes[...], 1)
    for at in tiles(result.shape):
        result[at] = pick([candidate[at] for candidate in candidates], masks)
    cells = result.shape[2]
    starts = [jnp.where(lax.axis_index("depth") == 0, cells - STEPS, 0)] if pair else [0, cells - STEPS]
    for start, edge in zip(starts, edges):
        for q in range(4):
            edge[q] = result[0, q, pl.ds(start, STEPS)]
        for q in range(3):
            edge[4 + q] = coefs[q][pl.ds(start, STEPS)]


def swap(x, way, phase):
    count, depth = lax.axis_size("dom"), lax.axis_size("depth")
    ways = ways_of(phase)
    pairs = [(i * depth + d, (i ^ ways[d % 2][way]) * depth + d) for i in range(count) for d in range(depth)]
    return lax.ppermute(x, ("dom", "depth"), pairs)


def local(ancestors, ensemble, diffusivity, melting_speed, permeability):
    count, depth = lax.axis_size("dom"), lax.axis_size("depth")
    sides = 1 << (count.bit_length() // 2)
    assert sides * sides == count
    far = range(1, sides)
    like = jax.ShapeDtypeStruct(ensemble.shape, jnp.float32)
    got = {k: swap(ensemble, k, 0) for k in far}
    coefs = (diffusivity, melting_speed, permeability)
    wish = pl.pallas_call(
        first_wishes_kernel,
        out_shape=jax.ShapeDtypeStruct((8, ensemble.shape[-1]), jnp.int32),
        in_specs=[SMEM],
        out_specs=VMEM,
        compiler_params=LIMIT,
        cost_estimate=FIRST_HOP,
        name="first_wishes",
    )(ancestors)
    candidates = [ensemble] + [got[k] for k in far]
    known, wishes, sent = 1, [wish], []
    while known < sides:
        wishes += [swap(wish, known, 1) for wish in wishes]
        known *= 2
    half = sides - sides // 4
    sent = choose(candidates, wishes[:half])
    if half < sides:
        sent += choose(candidates, wishes[half:])
    final = {k: swap(sent[k], k, 1) for k in far}
    edge = jax.ShapeDtypeStruct((7, STEPS) + ensemble.shape[3:], jnp.float32)
    edges = [edge] if depth == 2 else [edge, edge]
    state, *edges = pl.pallas_call(
        functools.partial(settle_kernel, sides, depth == 2),
        out_shape=[like] + edges,
        in_specs=[VMEM] * (sides + 4),
        out_specs=[VMEM] * (1 + len(edges)),
        compiler_params=LIMIT,
        name="settle",
    )(sent[0], *(final[k] for k in far), wish, *coefs)
    return forecast(state, edges, coefs)


def solution(mesh):
    return jax.shard_map(
        local,
        mesh=mesh,
        in_specs=(
            P("dom"),
            P("dom", None, "depth", None, None),
            P("depth", None, None),
            P("depth", None, None),
            P("depth", None, None),
        ),
        out_specs=P("dom", None, "depth", None, None),
        check_vma=False,
    )
```

```python
import functools
import itertools
import operator

import jax
import jax.numpy as jnp
from jax import lax
from jax.experimental import pallas as pl
from jax.experimental.pallas import tpu as pltpu
from jax.sharding import PartitionSpec as P

STEPS = 4
ADVECT = 0.1
SMEM = pl.BlockSpec(memory_space=pltpu.SMEM)
VMEM = pl.BlockSpec(memory_space=pltpu.VMEM)
FIRST_HOP = pl.CostEstimate(flops=10**10, bytes_accessed=8 * 10**6, transcendentals=0)
LIMIT = pltpu.CompilerParams(vmem_limit_bytes=32 * 1024 * 1024)


def neighbours(q):
    rows = lax.broadcasted_iota(jnp.int32, q.shape, 0)
    columns = lax.broadcasted_iota(jnp.int32, q.shape, 1)
    high_row, high_column = q.shape[0] - 1, q.shape[1] - 1
    total = jnp.where(rows == 0, 0.0, pltpu.roll(q, 1, 0))
    total = total + jnp.where(rows == high_row, 0.0, pltpu.roll(q, high_row, 0))
    total = total + jnp.where(columns == 0, 0.0, pltpu.roll(q, 1, 1))
    return total + jnp.where(columns == high_column, 0.0, pltpu.roll(q, high_column, 1))


def layer_step(state, layer, sign, diffuse, reacts, permeab):
    m, v, h, c = (state(q, layer) for q in range(4))
    m_up, v_up, h_up, c_up = (state(q, layer - 1) for q in range(4))
    m_low, v_low, h_low, c_low = (state(q, layer + 1) for q in range(4))
    speed = (ADVECT * sign) * v
    down, up = jnp.maximum(speed, 0.0), jnp.minimum(speed, 0.0)

    def transport(q, upper, lower):
        return down * (q - upper) + up * (lower - q)

    def laplace(q, upper, lower):
        return upper + lower + neighbours(q) - 6.0 * q

    melting = reacts * (h - 0.5 * c)
    return (
        m - transport(m, m_up, m_low) + melting,
        v + 0.2 * (permeab * jnp.tanh(m) - v) + 0.1 * laplace(v, v_up, v_low),
        h - transport(h, h_up, h_low) + diffuse * laplace(h, h_up, h_low) - 0.5 * melting,
        c - transport(c, c_up, c_low) + diffuse * laplace(c, c_up, c_low),
    )


def forecast_kernel(cells, count, own, d, r, p, low, high, out, even, odd, coefs):
    at = lax.axis_index("depth")
    window = cells + 2 * STEPS
    zero = jnp.zeros(even.shape[2:], jnp.float32)
    for q in range(4):
        for buffer in (even, odd):
            buffer[q, 0] = zero
            buffer[q, window + 1] = zero
    for q in range(7):
        to = even if q < 4 else coefs
        for i in range(STEPS):
            to[q % 4, 1 + i] = low[q, i]
            to[q % 4, 1 + STEPS + cells + i] = high[q, i]
        for i in range(cells):
            to[q % 4, 1 + STEPS + i] = own[0, q, i] if q < 4 else (d, r, p)[q - 4][i]
    inside_first = jnp.where(at == 0, 1 + STEPS, 0)
    inside_last = jnp.where(at == count - 1, STEPS + cells, window + 1)
    for step in range(STEPS):
        now, later = (even, odd) if step % 2 == 0 else (odd, even)
        for layer in range(2 + step, window - step):
            values = layer_step(lambda q, i: now[q, i], layer, 1.0, *(coefs[q, layer] for q in range(3)))
            for q in range(4):
                if step == STEPS - 1:
                    out[0, q, layer - STEPS - 1] = values[q]
                else:
                    inside = (layer >= inside_first) & (layer <= inside_last)
                    later[q, layer] = jnp.where(inside, values[q], 0.0)


def from_end(cells, i):
    return jnp.where(lax.axis_index("depth") == 0, i, cells - 1 - i)


def sign_of_order():
    return jnp.where(lax.axis_index("depth") == 0, 1.0, -1.0).astype(jnp.float32)


def inner_kernel(cells, own, d, r, p, head, border, even, odd):
    sign = sign_of_order()
    for q in range(4):
        for buffer in (even, odd):
            buffer[q, 0] = jnp.zeros(even.shape[2:], jnp.float32)
        for i in range(cells):
            even[q, 1 + i] = own[0, q, from_end(cells, i)]
    for step in range(STEPS):
        now, later = (even, odd) if step % 2 == 0 else (odd, even)
        layers = cells - 1 - step
        for layer in range(1, layers + 1):
            at = from_end(cells, layer - 1)
            values = layer_step(lambda q, i: now[q, i], layer, sign, d[at], r[at], p[at])
            for q in range(4):
                if step == STEPS - 1:
                    head[q, layer - 1] = values[q]
                    continue
                later[q, layer] = values[q]
                if layer > layers - 2:
                    border[step, q, layer - layers + 1] = values[q]


def outer_kernel(cells, own, d, r, p, other, head, border, out, state):
    sign = sign_of_order()
    for q in range(4):
        for i in range(2):
            state[0, q, i] = own[0, q, from_end(cells, cells - 2 + i)]
            for step in range(1, STEPS):
                state[step, q, i] = border[step - 1, q, i]
        for i in range(STEPS):
            state[0, q, 2 + i] = other[q, from_end(STEPS, i)]
        for i in range(cells - STEPS):
            out[0, q, from_end(cells, i)] = head[q, i]
    for step in range(STEPS):
        for i in range(1, 1 + STEPS):
            layer = cells - 1 - step + i
            if layer <= cells:
                at = from_end(cells, layer - 1)
                coefs = d[at], r[at], p[at]
            else:
                at = from_end(STEPS, layer - cells - 1)
                coefs = other[4, at], other[5, at], other[6, at]
            values = layer_step(lambda q, j: state[step, q, j], i, sign, *coefs)
            for q in range(4):
                if step == STEPS - 1:
                    out[0, q, from_end(cells, layer - 1)] = values[q]
                else:
                    state[step + 1, q, 1 + i] = values[q]


def other_side(x, towards):
    count = lax.axis_size("depth")
    if count == 2:
        return lax.ppermute(x, "depth", [(0, 1), (1, 0)])
    return lax.ppermute(x, "depth", [(i, i + towards) for i in range(count) if 0 <= i + towards < count])


def forecast(state, edges, coefs):
    count = lax.axis_size("depth")
    _, _, cells, rows, columns = state.shape
    assert cells >= STEPS
    result = jax.ShapeDtypeStruct(state.shape, jnp.float32)

    def layers(*lead):
        return lead + (rows, columns)

    def call(kernel, out_shape, scratch, *operands):
        return pl.pallas_call(
            kernel,
            out_shape=out_shape,
            in_specs=[VMEM] * len(operands),
            out_specs=jax.tree.map(lambda _: VMEM, out_shape),
            scratch_shapes=[pltpu.VMEM(shape, jnp.float32) for shape in scratch],
            compiler_params=LIMIT,
            name=kernel.func.__name__.removesuffix("_kernel"),
        )(*operands)

    if count == 2:
        other = other_side(edges[0], 1)
        parts = (
            jax.ShapeDtypeStruct(layers(4, max(cells - STEPS, 1)), jnp.float32),
            jax.ShapeDtypeStruct(layers(STEPS - 1, 4, 2), jnp.float32),
        )
        inner = functools.partial(inner_kernel, cells)
        head, border = call(inner, parts, [layers(4, cells + 1)] * 2, state, *coefs)
        outer = functools.partial(outer_kernel, cells)
        return call(outer, result, [layers(STEPS, 4, STEPS + 2)], state, *coefs, other, head, border)
    window = cells + 2 * STEPS + 2
    return call(
        functools.partial(forecast_kernel, cells, count),
        result,
        [layers(4, window), layers(4, window), layers(3, window)],
        state,
        *coefs,
        other_side(edges[1], 1),
        other_side(edges[0], -1),
    )


def first_wishes_kernel(mine, out):
    out[...] = jnp.full(out.shape, mine[0], jnp.int32)


def ways_of(phase):
    half = (lax.axis_size("dom").bit_length() - 1) // 2
    low = [1 << bit for bit in range(half)]
    high = [step << half for step in low]
    even, odd = (low[::-1], list(itertools.accumulate(high, operator.or_))) if phase == 0 else (high[::-1], low)
    ways = []
    for basis in (even, odd):
        offsets = [0]
        for step in basis:
            offsets += [offset ^ step for offset in offsets]
        ways.append(offsets)
    return ways


def hop_masks(wish, phase):
    even, odd = ways_of(phase)
    first = lax.axis_index("depth") % 2 == 0
    covered = jnp.where(first, functools.reduce(operator.or_, even), functools.reduce(operator.or_, odd))
    offset = (wish ^ lax.axis_index("dom")) & covered
    return [offset == jnp.where(first, *pair) for pair in list(zip(even, odd))[1:]]


def tiles(shape):
    return [(0, q, i, slice(r, r + 8)) for q in range(shape[1]) for i in range(shape[2]) for r in range(0, shape[3], 8)]


def pick(values, masks):
    value = values[0]
    for mask, other in zip(masks, values[1:]):
        value = jnp.where(mask, other, value)
    return value


def choose_kernel(sides, *refs):
    candidates, rest = refs[:sides], refs[sides:]
    wishes, results = rest[: len(rest) // 2], rest[len(rest) // 2 :]
    masks = [hop_masks(wish[...], 0) for wish in wishes]
    for at in tiles(candidates[0].shape):
        values = [candidate[at] for candidate in candidates]
        for mask, result in zip(masks, results):
            result[at] = pick(values, mask)


def choose(candidates, wishes):
    sides, outputs = len(candidates), len(wishes)
    return pl.pallas_call(
        functools.partial(choose_kernel, sides),
        out_shape=[jax.ShapeDtypeStruct(candidates[0].shape, jnp.float32)] * outputs,
        in_specs=[VMEM] * (sides + outputs),
        out_specs=[VMEM] * outputs,
        compiler_params=LIMIT,
        name="choose",
    )(*candidates, *wishes)


def settle_kernel(sides, pair, *refs):
    candidates, wishes, coefs = refs[:sides], refs[sides], refs[sides + 1 : sides + 4]
    result, edges = refs[sides + 4], refs[sides + 5 :]
    masks = hop_masks(wishes[...], 1)
    for at in tiles(result.shape):
        result[at] = pick([candidate[at] for candidate in candidates], masks)
    cells = result.shape[2]
    starts = [jnp.where(lax.axis_index("depth") == 0, cells - STEPS, 0)] if pair else [0, cells - STEPS]
    for start, edge in zip(starts, edges):
        for q in range(4):
            edge[q] = result[0, q, pl.ds(start, STEPS)]
        for q in range(3):
            edge[4 + q] = coefs[q][pl.ds(start, STEPS)]


def swap(x, way, phase):
    count, depth = lax.axis_size("dom"), lax.axis_size("depth")
    ways = ways_of(phase)
    pairs = [(i * depth + d, (i ^ ways[d % 2][way]) * depth + d) for i in range(count) for d in range(depth)]
    return lax.ppermute(x, ("dom", "depth"), pairs)


def local(ancestors, ensemble, diffusivity, melting_speed, permeability):
    count, depth = lax.axis_size("dom"), lax.axis_size("depth")
    sides = 1 << (count.bit_length() // 2)
    assert sides * sides == count
    far = range(1, sides)
    like = jax.ShapeDtypeStruct(ensemble.shape, jnp.float32)
    got = {k: swap(ensemble, k, 0) for k in far}
    coefs = (diffusivity, melting_speed, permeability)
    wish = pl.pallas_call(
        first_wishes_kernel,
        out_shape=jax.ShapeDtypeStruct((8, ensemble.shape[-1]), jnp.int32),
        in_specs=[SMEM],
        out_specs=VMEM,
        compiler_params=LIMIT,
        cost_estimate=FIRST_HOP,
        name="first_wishes",
    )(ancestors)
    candidates = [ensemble] + [got[k] for k in far]
    known, wishes, sent = 1, [wish], []
    while known < sides:
        wishes += [swap(wish, known, 1) for wish in wishes]
        known *= 2
    half = sides - sides // 4
    sent = choose(candidates, wishes[:half])
    if half < sides:
        sent += choose(candidates, wishes[half:])
    final = {k: swap(sent[k], k, 1) for k in far}
    edge = jax.ShapeDtypeStruct((7, STEPS) + ensemble.shape[3:], jnp.float32)
    edges = [edge] if depth == 2 else [edge, edge]
    state, *edges = pl.pallas_call(
        functools.partial(settle_kernel, sides, depth == 2),
        out_shape=[like] + edges,
        in_specs=[VMEM] * (sides + 4),
        out_specs=[VMEM] * (1 + len(edges)),
        compiler_params=LIMIT,
        name="settle",
    )(sent[0], *(final[k] for k in far), wish, *coefs)
    return forecast(state, edges, coefs)


def solution(mesh):
    return jax.shard_map(
        local,
        mesh=mesh,
        in_specs=(
            P("dom"),
            P("dom", None, "depth", None, None),
            P("depth", None, None),
            P("depth", None, None),
            P("depth", None, None),
        ),
        out_specs=P("dom", None, "depth", None, None),
        check_vma=False,
    )
```

```python
import functools
import itertools
import operator

import jax
import jax.numpy as jnp
from jax import lax
from jax.experimental import pallas as pl
from jax.experimental.pallas import tpu as pltpu
from jax.sharding import PartitionSpec as P

STEPS = 4
ADVECT = 0.1
SMEM = pl.BlockSpec(memory_space=pltpu.SMEM)
VMEM = pl.BlockSpec(memory_space=pltpu.VMEM)
FIRST_HOP = pl.CostEstimate(flops=10**10, bytes_accessed=8 * 10**6, transcendentals=0)
LIMIT = pltpu.CompilerParams(vmem_limit_bytes=32 * 1024 * 1024)


def neighbours(q):
    rows = lax.broadcasted_iota(jnp.int32, q.shape, 0)
    columns = lax.broadcasted_iota(jnp.int32, q.shape, 1)
    high_row, high_column = q.shape[0] - 1, q.shape[1] - 1
    total = jnp.where(rows == 0, 0.0, pltpu.roll(q, 1, 0))
    total = total + jnp.where(rows == high_row, 0.0, pltpu.roll(q, high_row, 0))
    total = total + jnp.where(columns == 0, 0.0, pltpu.roll(q, 1, 1))
    return total + jnp.where(columns == high_column, 0.0, pltpu.roll(q, high_column, 1))


def layer_step(state, layer, sign, diffuse, reacts, permeab):
    m, v, h, c = (state(q, layer) for q in range(4))
    m_up, v_up, h_up, c_up = (state(q, layer - 1) for q in range(4))
    m_low, v_low, h_low, c_low = (state(q, layer + 1) for q in range(4))
    speed = (ADVECT * sign) * v
    down, up = jnp.maximum(speed, 0.0), jnp.minimum(speed, 0.0)

    def transport(q, upper, lower):
        return down * (q - upper) + up * (lower - q)

    def laplace(q, upper, lower):
        return upper + lower + neighbours(q) - 6.0 * q

    melting = reacts * (h - 0.5 * c)
    return (
        m - transport(m, m_up, m_low) + melting,
        0.2 * (permeab * jnp.tanh(m) + v) + 0.1 * (v_up + v_low + neighbours(v)),
        h - transport(h, h_up, h_low) + diffuse * laplace(h, h_up, h_low) - 0.5 * melting,
        c - transport(c, c_up, c_low) + diffuse * laplace(c, c_up, c_low),
    )


def forecast_kernel(cells, count, own, d, r, p, low, high, out, even, odd, coefs):
    at = lax.axis_index("depth")
    window = cells + 2 * STEPS
    zero = jnp.zeros(even.shape[2:], jnp.float32)
    for q in range(4):
        for buffer in (even, odd):
            buffer[q, 0] = zero
            buffer[q, window + 1] = zero
    for q in range(7):
        to = even if q < 4 else coefs
        for i in range(STEPS):
            to[q % 4, 1 + i] = low[q, i]
            to[q % 4, 1 + STEPS + cells + i] = high[q, i]
        for i in range(cells):
            to[q % 4, 1 + STEPS + i] = own[0, q, i] if q < 4 else (d, r, p)[q - 4][i]
    inside_first = jnp.where(at == 0, 1 + STEPS, 0)
    inside_last = jnp.where(at == count - 1, STEPS + cells, window + 1)
    for step in range(STEPS):
        now, later = (even, odd) if step % 2 == 0 else (odd, even)
        for layer in range(2 + step, window - step):
            values = layer_step(lambda q, i: now[q, i], layer, 1.0, *(coefs[q, layer] for q in range(3)))
            for q in range(4):
                if step == STEPS - 1:
                    out[0, q, layer - STEPS - 1] = values[q]
                else:
                    inside = (layer >= inside_first) & (layer <= inside_last)
                    later[q, layer] = jnp.where(inside, values[q], 0.0)


def from_end(cells, i):
    return jnp.where(lax.axis_index("depth") == 0, i, cells - 1 - i)


def sign_of_order():
    return jnp.where(lax.axis_index("depth") == 0, 1.0, -1.0).astype(jnp.float32)


def inner_kernel(cells, own, d, r, p, head, border, even, odd):
    sign = sign_of_order()
    for q in range(4):
        for buffer in (even, odd):
            buffer[q, 0] = jnp.zeros(even.shape[2:], jnp.float32)
        for i in range(cells):
            even[q, 1 + i] = own[0, q, from_end(cells, i)]
    for step in range(STEPS):
        now, later = (even, odd) if step % 2 == 0 else (odd, even)
        layers = cells - 1 - step
        for layer in range(1, layers + 1):
            at = from_end(cells, layer - 1)
            values = layer_step(lambda q, i: now[q, i], layer, sign, d[at], r[at], p[at])
            for q in range(4):
                if step == STEPS - 1:
                    head[q, layer - 1] = values[q]
                    continue
                later[q, layer] = values[q]
                if layer > layers - 2:
                    border[step, q, layer - layers + 1] = values[q]


def outer_kernel(cells, own, d, r, p, other, head, border, out, state, result, sems):
    sign = sign_of_order()
    copies = []

    def leave(layer, values):
        for q in range(4):
            result[q, layer - 1] = values[q]
        to = out.at[0, :, from_end(cells, layer - 1)]
        copies.append(pltpu.make_async_copy(result.at[:, layer - 1], to, sems.at[layer - 1]))
        copies[-1].start()

    for layer in range(1, cells - STEPS + 1):
        leave(layer, [head[q, layer - 1] for q in range(4)])
    for q in range(4):
        for i in range(2):
            state[0, q, i] = own[0, q, from_end(cells, cells - 2 + i)]
            for step in range(1, STEPS):
                state[step, q, i] = border[step - 1, q, i]
        for i in range(STEPS):
            state[0, q, 2 + i] = other[q, from_end(STEPS, i)]
    for step in range(STEPS):
        for i in range(1, 1 + STEPS):
            layer = cells - 1 - step + i
            if layer <= cells:
                at = from_end(cells, layer - 1)
                coefs = d[at], r[at], p[at]
            else:
                at = from_end(STEPS, layer - cells - 1)
                coefs = other[4, at], other[5, at], other[6, at]
            values = layer_step(lambda q, j: state[step, q, j], i, sign, *coefs)
            if step == STEPS - 1:
                leave(layer, values)
                continue
            for q in range(4):
                state[step + 1, q, 1 + i] = values[q]
    for copy in copies:
        copy.wait()


def other_side(x, towards):
    count = lax.axis_size("depth")
    if count == 2:
        return lax.ppermute(x, "depth", [(0, 1), (1, 0)])
    return lax.ppermute(x, "depth", [(i, i + towards) for i in range(count) if 0 <= i + towards < count])


def forecast(state, edges, coefs):
    count = lax.axis_size("depth")
    _, _, cells, rows, columns = state.shape
    assert cells >= STEPS
    result = jax.ShapeDtypeStruct(state.shape, jnp.float32)

    def layers(*lead):
        return jax.ShapeDtypeStruct(lead + (rows, columns), jnp.float32)

    def held(*lead):
        return pltpu.VMEM(lead + (rows, columns), jnp.float32)

    def call(kernel, out_shape, scratch, *operands, space=VMEM):
        return pl.pallas_call(
            kernel,
            out_shape=out_shape,
            in_specs=[VMEM] * len(operands),
            out_specs=jax.tree.map(lambda _: space, out_shape),
            scratch_shapes=scratch,
            compiler_params=LIMIT,
            name=kernel.func.__name__.removesuffix("_kernel"),
        )(*operands)

    if count == 2:
        other = other_side(edges[0], 1)
        parts = (
            layers(4, max(cells - STEPS, 1)),
            layers(STEPS - 1, 4, 2),
        )
        inner = functools.partial(inner_kernel, cells)
        head, border = call(inner, parts, [held(4, cells + 1)] * 2, state, *coefs)
        outer = functools.partial(outer_kernel, cells)
        scratch = [held(STEPS, 4, STEPS + 2), held(4, cells), pltpu.SemaphoreType.DMA((cells,))]
        return call(outer, result, scratch, state, *coefs, other, head, border, space=pl.BlockSpec(memory_space=pl.ANY))
    window = cells + 2 * STEPS + 2
    return call(
        functools.partial(forecast_kernel, cells, count),
        result,
        [held(4, window), held(4, window), held(3, window)],
        state,
        *coefs,
        other_side(edges[1], 1),
        other_side(edges[0], -1),
    )


def first_wishes_kernel(mine, out):
    out[...] = jnp.full(out.shape, mine[0], jnp.int32)


def ways_of(phase):
    half = (lax.axis_size("dom").bit_length() - 1) // 2
    low = [1 << bit for bit in range(half)]
    high = [step << half for step in low]
    even, odd = (low[::-1], list(itertools.accumulate(high, operator.or_))) if phase == 0 else (high[::-1], low)
    ways = []
    for basis in (even, odd):
        offsets = [0]
        for step in basis:
            offsets += [offset ^ step for offset in offsets]
        ways.append(offsets)
    return ways


def hop_masks(wish, phase):
    even, odd = ways_of(phase)
    first = lax.axis_index("depth") % 2 == 0
    covered = jnp.where(first, functools.reduce(operator.or_, even), functools.reduce(operator.or_, odd))
    offset = (wish ^ lax.axis_index("dom")) & covered
    return [offset == jnp.where(first, *pair) for pair in list(zip(even, odd))[1:]]


def tiles(shape):
    return [(0, q, i, slice(r, r + 8)) for q in range(shape[1]) for i in range(shape[2]) for r in range(0, shape[3], 8)]


def pick(values, masks):
    value = values[0]
    for mask, other in zip(masks, values[1:]):
        value = jnp.where(mask, other, value)
    return value


def choose_kernel(sides, *refs):
    candidates, rest = refs[:sides], refs[sides:]
    wishes, results = rest[: len(rest) // 2], rest[len(rest) // 2 :]
    masks = [hop_masks(wish[...], 0) for wish in wishes]
    for at in tiles(candidates[0].shape):
        values = [candidate[at] for candidate in candidates]
        for mask, result in zip(masks, results):
            result[at] = pick(values, mask)


def choose(candidates, wishes):
    sides, outputs = len(candidates), len(wishes)
    return pl.pallas_call(
        functools.partial(choose_kernel, sides),
        out_shape=[jax.ShapeDtypeStruct(candidates[0].shape, jnp.float32)] * outputs,
        in_specs=[VMEM] * (sides + outputs),
        out_specs=[VMEM] * outputs,
        compiler_params=LIMIT,
        name="choose",
    )(*candidates, *wishes)


def settle_kernel(sides, pair, *refs):
    candidates, wishes, coefs = refs[:sides], refs[sides], refs[sides + 1 : sides + 4]
    result, edges = refs[sides + 4], refs[sides + 5 :]
    masks = hop_masks(wishes[...], 1)
    for at in tiles(result.shape):
        result[at] = pick([candidate[at] for candidate in candidates], masks)
    cells = result.shape[2]
    starts = [jnp.where(lax.axis_index("depth") == 0, cells - STEPS, 0)] if pair else [0, cells - STEPS]
    for start, edge in zip(starts, edges):
        for q in range(4):
            edge[q] = result[0, q, pl.ds(start, STEPS)]
        for q in range(3):
            edge[4 + q] = coefs[q][pl.ds(start, STEPS)]


def swap(x, way, phase):
    count, depth = lax.axis_size("dom"), lax.axis_size("depth")
    ways = ways_of(phase)
    pairs = [(i * depth + d, (i ^ ways[d % 2][way]) * depth + d) for i in range(count) for d in range(depth)]
    return lax.ppermute(x, ("dom", "depth"), pairs)


def local(ancestors, ensemble, diffusivity, melting_speed, permeability):
    count, depth = lax.axis_size("dom"), lax.axis_size("depth")
    sides = 1 << (count.bit_length() // 2)
    assert sides * sides == count
    far = range(1, sides)
    like = jax.ShapeDtypeStruct(ensemble.shape, jnp.float32)
    got = {k: swap(ensemble, k, 0) for k in far}
    coefs = (diffusivity, melting_speed, permeability)
    wish = pl.pallas_call(
        first_wishes_kernel,
        out_shape=jax.ShapeDtypeStruct((8, ensemble.shape[-1]), jnp.int32),
        in_specs=[SMEM],
        out_specs=VMEM,
        compiler_params=LIMIT,
        cost_estimate=FIRST_HOP,
        name="first_wishes",
    )(ancestors)
    candidates = [ensemble] + [got[k] for k in far]
    known, wishes, sent = 1, [wish], []
    while known < sides:
        wishes += [swap(wish, known, 1) for wish in wishes]
        known *= 2
    half = sides - sides // 4
    sent = choose(candidates, wishes[:half])
    if half < sides:
        sent += choose(candidates, wishes[half:])
    final = {k: swap(sent[k], k, 1) for k in far}
    edge = jax.ShapeDtypeStruct((7, STEPS) + ensemble.shape[3:], jnp.float32)
    edges = [edge] if depth == 2 else [edge, edge]
    state, *edges = pl.pallas_call(
        functools.partial(settle_kernel, sides, depth == 2),
        out_shape=[like] + edges,
        in_specs=[VMEM] * (sides + 4),
        out_specs=[VMEM] * (1 + len(edges)),
        compiler_params=LIMIT,
        name="settle",
    )(sent[0], *(final[k] for k in far), wish, *coefs)
    return forecast(state, edges, coefs)


def solution(mesh):
    return jax.shard_map(
        local,
        mesh=mesh,
        in_specs=(
            P("dom"),
            P("dom", None, "depth", None, None),
            P("depth", None, None),
            P("depth", None, None),
            P("depth", None, None),
        ),
        out_specs=P("dom", None, "depth", None, None),
        check_vma=False,
    )
```

```python
import functools
import itertools
import operator

import jax
import jax.numpy as jnp
from jax import lax
from jax.experimental import pallas as pl
from jax.experimental.pallas import tpu as pltpu
from jax.sharding import PartitionSpec as P

STEPS = 4
ADVECT = 0.1
SMEM = pl.BlockSpec(memory_space=pltpu.SMEM)
VMEM = pl.BlockSpec(memory_space=pltpu.VMEM)
FIRST_HOP = pl.CostEstimate(flops=10**10, bytes_accessed=8 * 10**6, transcendentals=0)
LIMIT = pltpu.CompilerParams(vmem_limit_bytes=32 * 1024 * 1024)


def neighbours(q):
    rows = lax.broadcasted_iota(jnp.int32, q.shape, 0)
    columns = lax.broadcasted_iota(jnp.int32, q.shape, 1)
    high_row, high_column = q.shape[0] - 1, q.shape[1] - 1
    total = jnp.where(rows == 0, 0.0, pltpu.roll(q, 1, 0))
    total = total + jnp.where(rows == high_row, 0.0, pltpu.roll(q, high_row, 0))
    total = total + jnp.where(columns == 0, 0.0, pltpu.roll(q, 1, 1))
    return total + jnp.where(columns == high_column, 0.0, pltpu.roll(q, high_column, 1))


def layer_step(state, layer, sign, diffuse, reacts, permeab):
    m, v, h, c = (state(q, layer) for q in range(4))
    m_up, v_up, h_up, c_up = (state(q, layer - 1) for q in range(4))
    m_low, v_low, h_low, c_low = (state(q, layer + 1) for q in range(4))
    speed = (ADVECT * sign) * v
    down, up = jnp.maximum(speed, 0.0), jnp.minimum(speed, 0.0)

    def transport(q, upper, lower):
        return down * (q - upper) + up * (lower - q)

    def laplace(q, upper, lower):
        return upper + lower + neighbours(q) - 6.0 * q

    melting = reacts * (h - 0.5 * c)
    return (
        m - transport(m, m_up, m_low) + melting,
        0.2 * (permeab * jnp.tanh(m) + v) + 0.1 * (v_up + v_low + neighbours(v)),
        h - transport(h, h_up, h_low) + diffuse * laplace(h, h_up, h_low) - 0.5 * melting,
        c - transport(c, c_up, c_low) + diffuse * laplace(c, c_up, c_low),
    )


def forecast_kernel(cells, count, own, d, r, p, low, high, out, even, odd, coefs):
    at = lax.axis_index("depth")
    window = cells + 2 * STEPS
    zero = jnp.zeros(even.shape[2:], jnp.float32)
    for q in range(4):
        for buffer in (even, odd):
            buffer[q, 0] = zero
            buffer[q, window + 1] = zero
    for q in range(7):
        to = even if q < 4 else coefs
        for i in range(STEPS):
            to[q % 4, 1 + i] = low[q, i]
            to[q % 4, 1 + STEPS + cells + i] = high[q, i]
        for i in range(cells):
            to[q % 4, 1 + STEPS + i] = own[0, q, i] if q < 4 else (d, r, p)[q - 4][i]
    inside_first = jnp.where(at == 0, 1 + STEPS, 0)
    inside_last = jnp.where(at == count - 1, STEPS + cells, window + 1)
    for step in range(STEPS):
        now, later = (even, odd) if step % 2 == 0 else (odd, even)
        for layer in range(2 + step, window - step):
            values = layer_step(lambda q, i: now[q, i], layer, 1.0, *(coefs[q, layer] for q in range(3)))
            for q in range(4):
                if step == STEPS - 1:
                    out[0, q, layer - STEPS - 1] = values[q]
                else:
                    inside = (layer >= inside_first) & (layer <= inside_last)
                    later[q, layer] = jnp.where(inside, values[q], 0.0)


def from_end(cells, i):
    return jnp.where(lax.axis_index("depth") == 0, i, cells - 1 - i)


def sign_of_order():
    return jnp.where(lax.axis_index("depth") == 0, 1.0, -1.0).astype(jnp.float32)


def inner_kernel(cells, own, d, r, p, head, border, even, odd):
    sign = sign_of_order()
    for q in range(4):
        for buffer in (even, odd):
            buffer[q, 0] = jnp.zeros(even.shape[2:], jnp.float32)
        for i in range(cells):
            even[q, 1 + i] = own[0, q, from_end(cells, i)]
    for step in range(STEPS):
        now, later = (even, odd) if step % 2 == 0 else (odd, even)
        layers = cells - 1 - step
        for layer in range(1, layers + 1):
            at = from_end(cells, layer - 1)
            values = layer_step(lambda q, i: now[q, i], layer, sign, d[at], r[at], p[at])
            for q in range(4):
                if step == STEPS - 1:
                    head[q, layer - 1] = values[q]
                    continue
                later[q, layer] = values[q]
                if layer > layers - 2:
                    border[step, q, layer - layers + 1] = values[q]


def outer_kernel(cells, own, d, r, p, other, head, border, out, state):
    sign = sign_of_order()
    for q in range(4):
        for i in range(2):
            state[0, q, i] = own[0, q, from_end(cells, cells - 2 + i)]
            for step in range(1, STEPS):
                state[step, q, i] = border[step - 1, q, i]
        for i in range(STEPS):
            state[0, q, 2 + i] = other[q, from_end(STEPS, i)]
        for i in range(cells - STEPS):
            out[0, q, from_end(cells, i)] = head[q, i]
    for step in range(STEPS):
        for i in range(1, 1 + STEPS):
            layer = cells - 1 - step + i
            if layer <= cells:
                at = from_end(cells, layer - 1)
                coefs = d[at], r[at], p[at]
            else:
                at = from_end(STEPS, layer - cells - 1)
                coefs = other[4, at], other[5, at], other[6, at]
            values = layer_step(lambda q, j: state[step, q, j], i, sign, *coefs)
            for q in range(4):
                if step == STEPS - 1:
                    out[0, q, from_end(cells, layer - 1)] = values[q]
                else:
                    state[step + 1, q, 1 + i] = values[q]


def other_side(x, towards):
    count = lax.axis_size("depth")
    if count == 2:
        return lax.ppermute(x, "depth", [(0, 1), (1, 0)])
    return lax.ppermute(x, "depth", [(i, i + towards) for i in range(count) if 0 <= i + towards < count])


def forecast(state, edges, coefs):
    count = lax.axis_size("depth")
    _, _, cells, rows, columns = state.shape
    assert cells >= STEPS
    result = jax.ShapeDtypeStruct(state.shape, jnp.float32)

    def layers(*lead):
        return lead + (rows, columns)

    def call(kernel, out_shape, scratch, *operands):
        return pl.pallas_call(
            kernel,
            out_shape=out_shape,
            in_specs=[VMEM] * len(operands),
            out_specs=jax.tree.map(lambda _: VMEM, out_shape),
            scratch_shapes=[pltpu.VMEM(shape, jnp.float32) for shape in scratch],
            compiler_params=LIMIT,
            name=kernel.func.__name__.removesuffix("_kernel"),
        )(*operands)

    if count == 2:
        other = other_side(edges[0], 1)
        parts = (
            jax.ShapeDtypeStruct(layers(4, max(cells - STEPS, 1)), jnp.float32),
            jax.ShapeDtypeStruct(layers(STEPS - 1, 4, 2), jnp.float32),
        )
        inner = functools.partial(inner_kernel, cells)
        head, border = call(inner, parts, [layers(4, cells + 1)] * 2, state, *coefs)
        outer = functools.partial(outer_kernel, cells)
        return call(outer, result, [layers(STEPS, 4, STEPS + 2)], state, *coefs, other, head, border)
    window = cells + 2 * STEPS + 2
    return call(
        functools.partial(forecast_kernel, cells, count),
        result,
        [layers(4, window), layers(4, window), layers(3, window)],
        state,
        *coefs,
        other_side(edges[1], 1),
        other_side(edges[0], -1),
    )


def first_wishes_kernel(mine, out):
    out[...] = jnp.full(out.shape, mine[0], jnp.int32)


def ways_of(phase):
    half = (lax.axis_size("dom").bit_length() - 1) // 2
    low = [1 << bit for bit in range(half)]
    high = [step << half for step in low]
    even, odd = (low[::-1], list(itertools.accumulate(high, operator.or_))) if phase == 0 else (high[::-1], low)
    ways = []
    for basis in (even, odd):
        offsets = [0]
        for step in basis:
            offsets += [offset ^ step for offset in offsets]
        ways.append(offsets)
    return ways


def hop_masks(wish, phase):
    even, odd = ways_of(phase)
    first = lax.axis_index("depth") % 2 == 0
    covered = jnp.where(first, functools.reduce(operator.or_, even), functools.reduce(operator.or_, odd))
    offset = (wish ^ lax.axis_index("dom")) & covered
    return [offset == jnp.where(first, *pair) for pair in list(zip(even, odd))[1:]]


def tiles(shape):
    return [(0, q, i, slice(r, r + 8)) for q in range(shape[1]) for i in range(shape[2]) for r in range(0, shape[3], 8)]


def pick(values, masks):
    value = values[0]
    for mask, other in zip(masks, values[1:]):
        value = jnp.where(mask, other, value)
    return value


def choose_kernel(sides, *refs):
    candidates, rest = refs[:sides], refs[sides:]
    wishes, results = rest[: len(rest) // 2], rest[len(rest) // 2 :]
    masks = [hop_masks(wish[...], 0) for wish in wishes]
    for at in tiles(candidates[0].shape):
        values = [candidate[at] for candidate in candidates]
        for mask, result in zip(masks, results):
            result[at] = pick(values, mask)


def choose(candidates, wishes):
    sides, outputs = len(candidates), len(wishes)
    return pl.pallas_call(
        functools.partial(choose_kernel, sides),
        out_shape=[jax.ShapeDtypeStruct(candidates[0].shape, jnp.float32)] * outputs,
        in_specs=[VMEM] * (sides + outputs),
        out_specs=[VMEM] * outputs,
        compiler_params=LIMIT,
        name="choose",
    )(*candidates, *wishes)


def settle_order(sides):
    return (1, *range(sides - 1, 1, -1))


def settle_kernel(sides, pair, *refs):
    candidates, wishes, coefs = refs[:sides], refs[sides], refs[sides + 1 : sides + 4]
    candidates = [candidates[(0, *settle_order(sides)).index(k)] for k in range(sides)]
    result, edges = refs[sides + 4], refs[sides + 5 :]
    masks = hop_masks(wishes[...], 1)
    for at in tiles(result.shape):
        result[at] = pick([candidate[at] for candidate in candidates], masks)
    cells = result.shape[2]
    starts = [jnp.where(lax.axis_index("depth") == 0, cells - STEPS, 0)] if pair else [0, cells - STEPS]
    for start, edge in zip(starts, edges):
        for q in range(4):
            edge[q] = result[0, q, pl.ds(start, STEPS)]
        for q in range(3):
            edge[4 + q] = coefs[q][pl.ds(start, STEPS)]


def swap(x, way, phase):
    count, depth = lax.axis_size("dom"), lax.axis_size("depth")
    ways = ways_of(phase)
    pairs = [(i * depth + d, (i ^ ways[d % 2][way]) * depth + d) for i in range(count) for d in range(depth)]
    return lax.ppermute(x, ("dom", "depth"), pairs)


def local(ancestors, ensemble, diffusivity, melting_speed, permeability):
    count, depth = lax.axis_size("dom"), lax.axis_size("depth")
    sides = 1 << (count.bit_length() // 2)
    assert sides * sides == count
    far = range(1, sides)
    like = jax.ShapeDtypeStruct(ensemble.shape, jnp.float32)
    got = {k: swap(ensemble, k, 0) for k in far}
    coefs = (diffusivity, melting_speed, permeability)
    wish = pl.pallas_call(
        first_wishes_kernel,
        out_shape=jax.ShapeDtypeStruct((8, ensemble.shape[-1]), jnp.int32),
        in_specs=[SMEM],
        out_specs=VMEM,
        compiler_params=LIMIT,
        cost_estimate=FIRST_HOP,
        name="first_wishes",
    )(ancestors)
    candidates = [ensemble] + [got[k] for k in far]
    known, wishes, sent = 1, [wish], []
    while known < sides:
        wishes += [swap(wish, known, 1) for wish in wishes]
        known *= 2
    half = sides - sides // 4
    sent = choose(candidates, wishes[:half])
    if half < sides:
        sent += choose(candidates, wishes[half:])
    final = {k: swap(sent[k], k, 1) for k in far}
    edge = jax.ShapeDtypeStruct((7, STEPS) + ensemble.shape[3:], jnp.float32)
    edges = [edge] if depth == 2 else [edge, edge]
    state, *edges = pl.pallas_call(
        functools.partial(settle_kernel, sides, depth == 2),
        out_shape=[like] + edges,
        in_specs=[VMEM] * (sides + 4),
        out_specs=[VMEM] * (1 + len(edges)),
        compiler_params=LIMIT,
        name="settle",
    )(sent[0], *(final[k] for k in settle_order(sides)), wish, *coefs)
    return forecast(state, edges, coefs)


def solution(mesh):
    return jax.shard_map(
        local,
        mesh=mesh,
        in_specs=(
            P("dom"),
            P("dom", None, "depth", None, None),
            P("depth", None, None),
            P("depth", None, None),
            P("depth", None, None),
        ),
        out_specs=P("dom", None, "depth", None, None),
        check_vma=False,
    )
```
